512 devices in a mesh: cell: 128 (over y, x, z_hi, core), gene: 4 (over z_lo).
Axes of the slice: x: 4, y: 4, z: 16 (z_hi: 4, z_lo: 4; z = z_hi * 4 + z_lo), core: 2. Of those that a mesh axis runs over, the one named last changes fastest.
Arguments:
- counts: bfloat16 [262144, 4096], P('cell', 'gene'), may hold values from -14 to 14
- loadings: bfloat16 [4096, 256], P('gene'), may hold values from -0.09375 to 0.09375
- kernel_widths: float32 [8], replicated, may hold values from 0.4 to 1.6
- width_index: int32 [262144], P(('cell', 'gene')), may hold values from 0 to 7
- block_fill: int32 [128], replicated, may hold values from 1 to 2048, 196608 in all
- plan: int32 [2], replicated, may hold values from 1 to 127, as said below
Outputs:
- density: float32 [262144], P(('cell', 'gene'))
- eccentricity: float32 [262144], P(('cell', 'gene'))
The draws below stay inside these ranges and needn't reach their ends.
Inputs may be any that keep to these rules, and one draw needn't show every extreme that they name: `plan`: the 2 values are distinct and one of them is 127.
All inputs are finite; a program needn't handle non-finite values.
Results may differ from the reference program's by a relative error of at most 0.00031.
Values may be sent and summed in bfloat16 or wider, within the bound.
No kernel may reach another device: no remote copies, remote signals or barrier semaphores. Data moves between devices by JAX's collectives and lax.ppermute only.
A program may use at most 64 MiB of HBM per device.

```python
import math
import jax
import jax.numpy as jnp
import numpy as np
from jax import lax

G = 4096
PC = 256
NWIDTH = 8
ROUNDS = 2
BLK = 2048
NBLOCKS = 128
CELLS = 262144


def draw_counts(key, part):
    key = jax.random.fold_in(key, 11)
    key_centre, key_label, key_noise, key_scale = jax.random.split(key, 4)
    centres = jnp.clip(jax.random.normal(key_centre, (48, G), jnp.float32), -4.0, 4.0)
    labels = jax.random.randint(key_label, (CELLS,), 0, 48).astype(jnp.int32)
    noise_scale = jnp.exp(jax.random.uniform(key_scale, (CELLS, 1), jnp.float32, jnp.log(0.25), jnp.log(0.75)))
    amplitude = jnp.full((48, 1), 2.0, jnp.float32)
    noise = jnp.clip(jax.random.normal(key_noise, (CELLS, G), jnp.float32), -4.0, 4.0)
    placed = (centres * amplitude)[labels]
    return (placed + noise_scale * noise).astype(jnp.bfloat16)


def draw_plan(key, part):
    key = jax.random.fold_in(key, 7)
    first, second = jax.random.split(key)
    other = jax.random.randint(first, (1,), 1, NBLOCKS - 1).astype(jnp.int32)
    far = jnp.full((1,), NBLOCKS - 1, jnp.int32)
    flip = jax.random.randint(second, (), 0, 2)
    return jnp.where(flip == 1, jnp.concatenate([far, other]), jnp.concatenate([other, far])).astype(jnp.int32)


def with_ends(entries, stream_key, least, top_value):
    index_at = [jax.random.randint(jax.random.fold_in(stream_key, axis), (), 0, length) for axis, length in enumerate(entries.shape)]
    main_axis = entries.shape.index(max(entries.shape))
    neighbour = index_at[:main_axis] + [(index_at[main_axis] + 1) % entries.shape[main_axis]] + index_at[main_axis + 1:]
    return entries.at[tuple(index_at)].set(least).at[tuple(neighbour)].set(top_value)


def levels(stream_key, shape, pieces, least, largest):
    factor_of = 1.0
    for position, parts in pieces:
        heights = jax.random.uniform(jax.random.fold_in(jax.random.fold_in(stream_key, 6), position), (parts,), jnp.float32, least / len(pieces), largest / len(pieces))
        factor_of = factor_of * jnp.repeat(jnp.exp(heights), shape[position] // parts).reshape((-1,) + (1,) * (len(shape) - 1 - position))
    return factor_of


def profile(amount, total, bound, slope):
    loads = [(1 << 20) // math.isqrt(rank ** slope) + 1 for rank in range(2, amount + 1)]
    rest, holding = total - bound - (amount - 1), [1] * (amount - 1)
    while rest > 0:
        free = [i for i in range(amount - 1) if holding[i] < bound]
        pool, budget = sum([loads[i] for i in free]), rest
        for i in free:
            addition = min(bound - holding[i], max(1, budget * loads[i] // pool), rest)
            holding[i] = holding[i] + addition
            rest = rest - addition
    return np.array([bound] + holding)


def ragged_sizes(stream_key, number_of, total, bound, lean):
    if number_of == 2:
        one = jax.random.randint(stream_key, (), max(1, total - bound), min(bound, total - 1) + 1)
        return jnp.stack([one, total - one])
    sizes = jnp.asarray(profile(number_of, total, bound, lean), jnp.int32)
    twos = (number_of - 1) // 2
    donor, receiver = sizes[1:1 + 2 * twos:2], sizes[2:2 + 2 * twos:2]
    margin = jnp.minimum(donor - 1, bound - receiver)
    passed = jax.random.randint(jax.random.fold_in(stream_key, 1), (twos,), 0, 1 << 20) % (margin + 1)
    sizes = sizes.at[1:1 + 2 * twos:2].set(donor - passed).at[2:2 + 2 * twos:2].set(receiver + passed)
    return sizes[jax.random.permutation(jax.random.fold_in(stream_key, 2), number_of)]


def normal_values(own_key, extent, scale, limit, pieces=(), held_as=jnp.bfloat16):
    loudness = levels(own_key, extent, pieces, -0.22, 0.18) if pieces else 1.0
    array = jax.random.normal(own_key, extent, jnp.float32) * scale * loudness
    return jnp.minimum(jnp.maximum(array, -limit), limit).astype(held_as)


def setup_inputs(seed: int = 0) -> dict:
    splits = jax.random.split(jax.random.key(seed), 7)
    return {
        "counts": draw_counts(jax.random.fold_in(splits[6], 71), 0),
        "loadings": normal_values(splits[1], (G, PC), G ** -0.5, 0.09375, ((0, 4),)),
        "kernel_widths": jnp.clip(jnp.exp(jax.random.uniform(splits[2], (NWIDTH,), jnp.float32, math.log(0.4), math.log(1.6))), 0.4, 1.6),
        "width_index": with_ends(jax.random.randint(splits[3], (CELLS,), 0, NWIDTH), jax.random.fold_in(splits[3], 1), 0, NWIDTH - 1).astype(jnp.int32),
        "block_fill": ragged_sizes(splits[4], NBLOCKS, NBLOCKS * BLK * 3 // 4, BLK, 1).astype(jnp.int32),
        "plan": draw_plan(jax.random.fold_in(splits[6], 71), 0),
    }


def block_terms(queries, coef, keys, fill):
    qf = queries.astype(jnp.float32)
    kf = keys.astype(jnp.float32)
    qnorm = lax.optimization_barrier(jnp.sum(qf * qf, axis=1))
    knorm = lax.optimization_barrier(jnp.sum(kf * kf, axis=1))
    inner = jnp.einsum('qc,kc->qk', qf, kf, precision=lax.Precision.HIGHEST)
    dist = jnp.maximum(qnorm[:, None] + knorm[None, :] - 2.0 * inner, 0.0)
    live = jnp.arange(keys.shape[0], dtype=jnp.int32)[None, :] < fill
    kernel = jnp.where(live, jnp.exp(-dist * coef[:, None]), 0.0)
    return (lax.optimization_barrier(jnp.sum(kernel, axis=1)), lax.optimization_barrier(jnp.max(jnp.where(live, dist, 0.0), axis=1)))

def reference(counts, loadings, kernel_widths, width_index, block_fill, plan):
    scores = jnp.dot(counts, loadings, preferred_element_type=jnp.float32).astype(jnp.bfloat16)
    blocks = scores.reshape(NBLOCKS, BLK, PC)
    picked = width_index[:, None] == jnp.arange(NWIDTH, dtype=jnp.int32)[None, :]
    width = lax.optimization_barrier(jnp.sum(jnp.where(picked, kernel_widths[None, :], 0.0), axis=1))
    coef = (1.0 / (2.0 * PC * width * width)).reshape(NBLOCKS, BLK)

    def one_block(index):
        queries = blocks[index]
        total, top = block_terms(queries, coef[index], queries, block_fill[index])
        for step in range(ROUNDS):
            other = jnp.bitwise_xor(index, plan[step]).astype(jnp.int32)
            more, far = block_terms(queries, coef[index], blocks[other], block_fill[other])
            total = total + more
            top = jnp.maximum(top, far)
        qlive = jnp.arange(BLK, dtype=jnp.int32) < block_fill[index]
        density = jnp.where(qlive, jnp.log(total), 0.0)
        spread = jnp.where(qlive, jnp.sqrt(top / PC), 0.0)
        return (density, spread)
    density, spread = lax.map(one_block, jnp.arange(NBLOCKS, dtype=jnp.int32))
    return (density.reshape(CELLS), spread.reshape(CELLS))
```

```python
import jax
import jax.numpy as jnp
from jax import lax
from jax.sharding import PartitionSpec as P


def swapped(value, axis, mask):
    pairs = [(source, source ^ mask) for source in range(lax.axis_size(axis))]
    return lax.ppermute(value, axis, pairs)


def block_terms(queries, coef, keys, first, fill):
    qf = queries.astype(jnp.float32)
    kf = keys.astype(jnp.float32)
    qnorm = jnp.sum(qf * qf, axis=1)
    knorm = jnp.sum(kf * kf, axis=1)
    inner = jnp.einsum("qc,kc->qk", queries, keys, preferred_element_type=jnp.float32)
    dist = jnp.maximum(qnorm[:, None] + knorm[None, :] - 2.0 * inner, 0.0)
    live = first + jnp.arange(keys.shape[0], dtype=jnp.int32)[None, :] < fill
    kernel = jnp.where(live, jnp.exp(-dist * coef[:, None]), 0.0)
    return (jnp.sum(kernel, axis=1), jnp.max(jnp.where(live, dist, 0.0), axis=1))


def lookup(table, index):
    slots = jnp.arange(table.shape[0], dtype=jnp.int32)
    return jnp.sum(jnp.where(slots == index, table, 0))


def per_device(counts, loadings, kernel_widths, width_index, block_fill, plan):
    groups = lax.axis_size("gene")
    blocks = lax.axis_size("cell")
    rows = counts.shape[0]
    share = rows // groups
    gene_pos = lax.axis_index("gene")
    cell_pos = lax.axis_index("cell")
    comps = loadings.shape[1]
    far = blocks - 1
    other = jnp.where(plan[0] == far, plan[1], plan[0])

    picked = width_index[:, None] == jnp.arange(kernel_widths.shape[0], dtype=jnp.int32)[None, :]
    width = jnp.sum(jnp.where(picked, kernel_widths[None, :], 0.0), axis=1)
    coef = 1.0 / (2.0 * comps * width * width)
    coefs = [coef] + [swapped(coef, "gene", d) for d in range(1, groups)]

    def part(position):
        mine = lax.dynamic_slice_in_dim(counts, position * share, share, 0)
        return jnp.dot(mine, loadings, preferred_element_type=jnp.float32)

    arrived = []
    for d in range(groups - 1, 0, -1):
        leaving = part(jnp.bitwise_xor(gene_pos, d)).astype(jnp.float16)
        arrived.append(swapped(leaving, "gene", d))
    summed = part(gene_pos)
    for piece in arrived:
        summed = summed + piece.astype(jnp.float32)
    scores = summed.astype(jnp.bfloat16)

    partner = swapped(scores, "cell", far)
    queries = [scores] + [swapped(scores, "gene", d) for d in range(1, groups)]
    moves = [lambda x, mask=mask: swapped(x, "cell", mask) for mask in range(1, far)]
    second = lax.switch(other - 1, moves, scores)

    own_fill = lookup(block_fill, cell_pos)
    far_fill = lookup(block_fill, jnp.bitwise_xor(cell_pos, far))
    other_fill = lookup(block_fill, jnp.bitwise_xor(cell_pos, other))
    first = gene_pos * share
    sums, tops = [], []
    for q, c in zip(queries, coefs):
        total, top = block_terms(q, c, scores, first, own_fill)
        for keys, fill in ((partner, far_fill), (second, other_fill)):
            more, wide = block_terms(q, c, keys, first, fill)
            total = total + more
            top = jnp.maximum(top, wide)
        sums.append(total)
        tops.append(top)
    total, top = sums[0], tops[0]
    for d in range(1, groups):
        back = swapped(jnp.stack([sums[d], tops[d]]), "gene", d)
        total = total + back[0]
        top = jnp.maximum(top, back[1])

    qlive = first + jnp.arange(share, dtype=jnp.int32) < own_fill
    density = jnp.where(qlive, jnp.log(total), 0.0)
    spread = jnp.where(qlive, jnp.sqrt(top / comps), 0.0)
    return (density, spread)


def solution(mesh):
    placed = (P("cell", "gene"), P("gene", None), P(), P(("cell", "gene")), P(), P())
    return jax.shard_map(
        per_device,
        mesh=mesh,
        in_specs=placed,
        out_specs=(P(("cell", "gene")), P(("cell", "gene"))),
        check_vma=False,
    )
```

```python
import functools

import jax
import jax.numpy as jnp
from jax import lax
from jax.experimental import pallas as pl
from jax.experimental.pallas import tpu as pltpu
from jax.sharding import PartitionSpec as P

EXTRA = 16
BIG = 1e30
LOG2E = 1.4426950408889634


def swapped(value, axis, mask):
    pairs = [(source, source ^ mask) for source in range(lax.axis_size(axis))]
    return lax.ppermute(value, axis, pairs)


def chosen(value, axis, index, unit, count):
    moves = [lambda x: x]
    for step in range(1, count):
        moves.append(lambda x, mask=step * unit: swapped(x, axis, mask))
    return lax.switch(index, moves, value)


def squares(x):
    xf = x.astype(jnp.float32)
    square = xf * xf
    high = square.astype(jnp.bfloat16)
    low = (square - high.astype(jnp.float32)).astype(jnp.bfloat16)
    return high, low


def across(a, b):
    return lax.dot_general(a, b, (((1,), (1,)), ((), ())), preferred_element_type=jnp.float32)


def terms_kernel(share, comps, where_ref, fill_ref, widths_ref, query_ref, own_ref, far_ref, other_ref, out_ref, near_ref, wide_ref, twice_ref):
    first = where_ref[0]
    keys = (own_ref, far_ref, other_ref)

    @pl.when(pl.program_id(0) == 0)
    def _():
        ones = jnp.ones((128, comps), jnp.bfloat16)
        slot = first + lax.broadcasted_iota(jnp.int32, (share, 128), 0)
        for n, key_ref in enumerate(keys):
            block = key_ref[...]
            high, low = squares(block)
            norm = across(high, ones) + across(low, ones)
            live = slot < fill_ref[where_ref[1 + n]]
            near_ref[n] = jnp.where(live, norm, BIG)
            wide_ref[n] = jnp.where(live, norm, -BIG)
            twice_ref[n] = block * jnp.bfloat16(-2)

    query = query_ref[0, :share, :]
    high, low = squares(query)
    ones = jnp.ones((8, comps), jnp.bfloat16)
    norm = (across(ones, high) + across(ones, low))[:1]
    index = query_ref[0, share:, :].astype(jnp.float32)
    index = jnp.concatenate([index[row : row + 1] for row in range(share // comps)], axis=1)
    width = jnp.zeros((1, share), jnp.float32)
    for n in range(widths_ref.shape[0]):
        width = jnp.where(index == float(n), widths_ref[n], width)
    coef = -LOG2E / (2.0 * comps * width * width)

    total = jnp.zeros((8, share), jnp.float32)
    top = jnp.full((8, share), -BIG, jnp.float32)
    for n in range(len(keys)):
        inner = across(twice_ref[n], query)
        near = jnp.concatenate([near_ref[n]] * (share // 128), axis=1)
        wide = jnp.concatenate([wide_ref[n]] * (share // 128), axis=1)
        dist = jnp.maximum(inner + near + norm, 0.0)
        kernel = jnp.exp2(dist * coef)
        total = total + jnp.sum(kernel.reshape(share // 8, 8, share), axis=0)
        top = jnp.maximum(top, jnp.max((inner + wide).reshape(share // 8, 8, share), axis=0))
    out_ref[0, 0:1, :] = jnp.sum(total, axis=0, keepdims=True)
    out_ref[0, 1:2, :] = jnp.maximum(jnp.max(top, axis=0, keepdims=True) + norm, 0.0)


def block_terms(where, fill, widths, queries, own, far, other):
    groups, padded, comps = queries.shape
    share = own.shape[0]
    whole = pl.BlockSpec((share, comps), lambda j: (0, 0))
    smem = pl.BlockSpec(memory_space=pltpu.SMEM)
    return pl.pallas_call(
        functools.partial(terms_kernel, share, comps),
        grid=(groups,),
        out_shape=jax.ShapeDtypeStruct((groups, 2, share), jnp.float32),
        in_specs=[smem, smem, smem, pl.BlockSpec((1, padded, comps), lambda j: (j, 0, 0)), whole, whole, whole],
        out_specs=pl.BlockSpec((1, 2, share), lambda j: (j, 0, 0)),
        scratch_shapes=[
            pltpu.VMEM((3, share, 128), jnp.float32),
            pltpu.VMEM((3, share, 128), jnp.float32),
            pltpu.VMEM((3, share, comps), jnp.bfloat16),
        ],
        compiler_params=pltpu.CompilerParams(vmem_limit_bytes=32 * 1024 * 1024),
    )(where, fill, widths, queries, own, far, other)


def per_device(counts, loadings, kernel_widths, width_index, block_fill, plan):
    groups = lax.axis_size("gene")
    blocks = lax.axis_size("cell")
    rows = counts.shape[0]
    share = rows // groups
    gene_pos = lax.axis_index("gene")
    cell_pos = lax.axis_index("cell")
    comps = loadings.shape[1]
    far = blocks - 1
    other = jnp.where(plan[0] == far, plan[1], plan[0])
    first = gene_pos * share
    where = jnp.stack([first, cell_pos, jnp.bitwise_xor(cell_pos, far), jnp.bitwise_xor(cell_pos, other)])

    def part(shard, chunk):
        begin = jnp.bitwise_xor(gene_pos, shard) * share + chunk * half
        mine = lax.dynamic_slice_in_dim(counts, begin, half, 0)
        return jnp.dot(mine, loadings, preferred_element_type=jnp.float32)

    def narrow(x):
        return lax.reduce_precision(x, 8, 10).astype(jnp.float16)

    chunks = 2
    half = share // chunks
    near = [swapped(jnp.concatenate([narrow(part(1, c)), narrow(part(3, c))]), "gene", 1) for c in range(chunks)]
    kept = [(part(0, c), part(2, c)) for c in range(chunks)]
    wide = [swapped(narrow(kept[c][1] + near[c][half:].astype(jnp.float32)), "gene", 2) for c in range(chunks)]
    summed = jnp.concatenate([kept[c][0] + near[c][:half].astype(jnp.float32) + wide[c].astype(jnp.float32) for c in range(chunks)])
    scores = summed.astype(jnp.bfloat16)

    index = jnp.pad(width_index.astype(jnp.bfloat16).reshape(-1, comps), ((0, EXTRA - share // comps), (0, 0)))
    partner = swapped(scores, "cell", far)
    message = jnp.concatenate([scores, index], axis=0)
    queries = lax.all_to_all(jnp.broadcast_to(message[None], (groups,) + message.shape), "gene", 0, 0)
    low = 8
    second = chosen(scores, "cell", other // low, low, blocks // low)
    second = chosen(second, "cell", other % low, 1, low)

    terms = block_terms(where, block_fill, kernel_widths, queries, scores, partner, second)
    both = lax.all_to_all(terms, "gene", 0, 0)
    total = jnp.sum(both[:, 0], axis=0)
    top = jnp.max(both[:, 1], axis=0)
    qlive = first + jnp.arange(share, dtype=jnp.int32) < block_fill[cell_pos]
    density = jnp.where(qlive, jnp.log(total), 0.0)
    spread = jnp.where(qlive, jnp.sqrt(top / comps), 0.0)
    return (density, spread)


def solution(mesh):
    placed = (P("cell", "gene"), P("gene", None), P(), P(("cell", "gene")), P(), P())
    return jax.shard_map(
        per_device,
        mesh=mesh,
        in_specs=placed,
        out_specs=(P(("cell", "gene")), P(("cell", "gene"))),
        check_vma=False,
    )
```

```python
import functools

import jax
import jax.numpy as jnp
from jax import lax
from jax.experimental import pallas as pl
from jax.experimental.pallas import tpu as pltpu
from jax.sharding import PartitionSpec as P

EXTRA = 16
BIG = 1e30
LOG2E = 1.4426950408889634


def swapped(value, axis, mask):
    pairs = [(source, source ^ mask) for source in range(lax.axis_size(axis))]
    return lax.ppermute(value, axis, pairs)


def chosen(value, axis, index, unit, count):
    moves = [lambda x: x]
    for step in range(1, count):
        moves.append(lambda x, mask=step * unit: swapped(x, axis, mask))
    return lax.switch(index, moves, value)


def squares(x):
    xf = x.astype(jnp.float32)
    square = xf * xf
    high = square.astype(jnp.bfloat16)
    low = (square - high.astype(jnp.float32)).astype(jnp.bfloat16)
    return high, low


def across(a, b):
    return lax.dot_general(a, b, (((1,), (1,)), ((), ())), preferred_element_type=jnp.float32)


def terms_kernel(share, comps, where_ref, fill_ref, widths_ref, mine_ref, second_ref, beside_ref, across_ref, own_ref, far_ref, other_ref, out_ref, near_ref, wide_ref, twice_ref):
    first = where_ref[0] * share
    keys = (own_ref, far_ref, other_ref)
    ones = jnp.ones((128, comps), jnp.bfloat16)
    slot = first + lax.broadcasted_iota(jnp.int32, (share, 128), 0)
    for n, key_ref in enumerate(keys):
        block = key_ref[...]
        high, low = squares(block)
        norm = across(high, ones) + across(low, ones)
        live = slot < fill_ref[where_ref[1 + n]]
        near_ref[n] = jnp.where(live, norm, BIG)
        wide_ref[n] = jnp.where(live, norm, -BIG)
        twice_ref[n] = block * jnp.bfloat16(-2)

    lanes = 256
    def step(query_ref, shard, begin):
        query = query_ref[pl.ds(begin, lanes), :]
        high, low = squares(query)
        few = jnp.ones((8, comps), jnp.bfloat16)
        norm = (across(few, high) + across(few, low))[:1]
        index = query_ref[share:, :].astype(jnp.float32)
        index = jnp.concatenate([index[row : row + 1] for row in range(begin // comps, (begin + lanes) // comps)], axis=1)
        width = jnp.zeros((1, lanes), jnp.float32)
        for n in range(widths_ref.shape[0]):
            width = jnp.where(index == float(n), widths_ref[n], width)
        coef = -LOG2E / (2.0 * comps * width * width)
        total = jnp.zeros((8, lanes), jnp.float32)
        top = jnp.full((8, lanes), -BIG, jnp.float32)
        for n in range(len(keys)):
            inner = across(twice_ref[n], query)
            near = jnp.concatenate([near_ref[n]] * (lanes // 128), axis=1)
            wide = jnp.concatenate([wide_ref[n]] * (lanes // 128), axis=1)
            dist = jnp.maximum(inner + near + norm, 0.0)
            kernel = jnp.exp2(dist * coef)
            total = total + jnp.sum(kernel.reshape(share // 8, 8, lanes), axis=0)
            top = jnp.maximum(top, jnp.max((inner + wide).reshape(share // 8, 8, lanes), axis=0))
        out_ref[shard, 0:1, pl.ds(begin, lanes)] = jnp.sum(total, axis=0, keepdims=True)
        out_ref[shard, 1:2, pl.ds(begin, lanes)] = jnp.maximum(jnp.max(top, axis=0, keepdims=True) + norm, 0.0)

    for ref, flip in ((mine_ref, 0), (second_ref, 2), (beside_ref, 1), (across_ref, 3)):
        shard = jnp.bitwise_xor(where_ref[0], flip)
        for begin in range(0, share, lanes):
            step(ref, shard, begin)


def block_terms(where, fill, widths, mine, beside, own, far, other):
    share, comps = own.shape
    groups = len(mine) + len(beside)
    whole = pl.BlockSpec(memory_space=pltpu.VMEM)
    smem = pl.BlockSpec(memory_space=pltpu.SMEM)
    return pl.pallas_call(
        functools.partial(terms_kernel, share, comps),
        out_shape=jax.ShapeDtypeStruct((groups, 2, share), jnp.float32),
        in_specs=[smem] * 3 + [whole] * 7,
        out_specs=whole,
        scratch_shapes=[
            pltpu.VMEM((3, share, 128), jnp.float32),
            pltpu.VMEM((3, share, 128), jnp.float32),
            pltpu.VMEM((3, share, comps), jnp.bfloat16),
        ],
        compiler_params=pltpu.CompilerParams(vmem_limit_bytes=32 * 1024 * 1024),
    )(where, fill, widths, *mine, *beside, own, far, other)


def per_device(counts, loadings, kernel_widths, width_index, block_fill, plan):
    groups = lax.axis_size("gene")
    blocks = lax.axis_size("cell")
    rows = counts.shape[0]
    share = rows // groups
    gene_pos = lax.axis_index("gene")
    cell_pos = lax.axis_index("cell")
    comps = loadings.shape[1]
    far = blocks - 1
    other = jnp.where(plan[0] == far, plan[1], plan[0])
    where = jnp.stack([gene_pos, cell_pos, jnp.bitwise_xor(cell_pos, far), jnp.bitwise_xor(cell_pos, other)])
    first = gene_pos * share
    forward = jnp.bitwise_and(other, 4) != 0
    path = jnp.where(forward, jnp.bitwise_xor(other, far), other)
    early = jnp.where(forward, 0, path % 4)
    late = jnp.where(forward, path % 4, 0)
    across_plane = path // 8
    index = jnp.pad(width_index.reshape(-1, comps), ((0, EXTRA - share // comps), (0, 0)))

    chunks = 2
    half = share // chunks

    def partial(shard, chunk):
        begin = jnp.bitwise_xor(gene_pos, shard) * share + chunk * half
        rows = lax.dynamic_slice_in_dim(counts, begin, half, 0)
        return jnp.dot(rows, loadings, preferred_element_type=jnp.float32)

    def narrow(x):
        return lax.reduce_precision(x, 8, 10).astype(jnp.float16)

    def widen(x):
        return x.astype(jnp.float32)

    near = [swapped(jnp.concatenate([narrow(partial(1, c)), narrow(partial(3, c))]), "gene", 1) for c in range(chunks)]
    pair = [
        (narrow(partial(0, c) + widen(near[c][:half])), narrow(partial(2, c) + widen(near[c][half:])))
        for c in range(chunks)
    ]
    wide = [swapped(pair[c][1], "gene", 2) for c in range(chunks)]
    back = swapped(jnp.concatenate([pair[c][0] for c in range(chunks)] + [index.astype(jnp.float16)]), "gene", 2)
    wide[0], forward, early, late, across_plane, where = lax.optimization_barrier((wide[0], forward, early, late, across_plane, where))
    scores = jnp.concatenate([widen(pair[c][0]) + widen(wide[c]) for c in range(chunks)]).astype(jnp.bfloat16)
    partner = swapped(scores, "cell", far)
    moved = chosen(scores, "cell", early, 1, 4)
    back, moved = lax.optimization_barrier((back, moved))
    second = jnp.concatenate([widen(pair[c][1]) + widen(back[c * half : (c + 1) * half]) for c in range(chunks)]).astype(jnp.bfloat16)
    mine = [
        jnp.concatenate([scores, index.astype(jnp.bfloat16)]),
        jnp.concatenate([second, back[share:].astype(jnp.bfloat16)]),
    ]
    beside = [swapped(part, "gene", 1) for part in mine]
    moved = jnp.where(forward, partner, moved)
    moved = chosen(moved, "cell", late, 1, 4)
    moved = chosen(moved, "cell", across_plane, 8, blocks // 8)

    terms = block_terms(where, block_fill, kernel_widths, mine, beside, scores, partner, moved)
    both = lax.all_to_all(terms, "gene", 0, 0)
    total = jnp.sum(both[:, 0], axis=0)
    top = jnp.max(both[:, 1], axis=0)
    qlive = first + jnp.arange(share, dtype=jnp.int32) < block_fill[cell_pos]
    density = jnp.where(qlive, jnp.log(total), 0.0)
    spread = jnp.where(qlive, jnp.sqrt(top / comps), 0.0)
    return (density, spread)


def solution(mesh):
    placed = (P("cell", "gene"), P("gene", None), P(), P(("cell", "gene")), P(), P())
    return jax.shard_map(
        per_device,
        mesh=mesh,
        in_specs=placed,
        out_specs=(P(("cell", "gene")), P(("cell", "gene"))),
        check_vma=False,
    )
```

```python
import functools

import jax
import jax.numpy as jnp
from jax import lax
from jax.experimental import pallas as pl
from jax.experimental.pallas import tpu as pltpu
from jax.sharding import PartitionSpec as P

EXTRA = 16
BIG = 1e30
LOG2E = 1.4426950408889634


def swapped(value, axis, mask):
    pairs = [(source, source ^ mask) for source in range(lax.axis_size(axis))]
    return lax.ppermute(value, axis, pairs)


def chosen(value, axis, index, unit, count):
    moves = [lambda x: x]
    for step in range(1, count):
        moves.append(lambda x, mask=step * unit: swapped(x, axis, mask))
    return lax.switch(index, moves, value)


def squares(x):
    xf = x.astype(jnp.float32)
    square = xf * xf
    high = square.astype(jnp.bfloat16)
    low = (square - high.astype(jnp.float32)).astype(jnp.bfloat16)
    return high, low


def across(a, b):
    return lax.dot_general(a, b, (((1,), (1,)), ((), ())), preferred_element_type=jnp.float32)


def terms_kernel(share, comps, where_ref, fill_ref, widths_ref, mine_ref, second_ref, beside_ref, across_ref, own_ref, far_ref, other_ref, out_ref, near_ref, wide_ref, twice_ref):
    first = where_ref[0] * share
    keys = (own_ref, far_ref, other_ref)
    ones = jnp.ones((128, comps), jnp.bfloat16)
    slot = first + lax.broadcasted_iota(jnp.int32, (share, 128), 0)
    for n, key_ref in enumerate(keys):
        block = key_ref[...]
        high, low = squares(block)
        norm = across(high, ones) + across(low, ones)
        live = slot < fill_ref[where_ref[1 + n]]
        near_ref[n] = jnp.where(live, norm, BIG)
        wide_ref[n] = jnp.where(live, norm, -BIG)
        twice_ref[n] = block * jnp.bfloat16(-2)

    lanes = 256
    def step(query_ref, shard, begin):
        query = query_ref[pl.ds(begin, lanes), :]
        high, low = squares(query)
        few = jnp.ones((8, comps), jnp.bfloat16)
        norm = (across(few, high) + across(few, low))[:1]
        index = query_ref[share:, :].astype(jnp.float32)
        index = jnp.concatenate([index[row : row + 1] for row in range(begin // comps, (begin + lanes) // comps)], axis=1)
        width = jnp.zeros((1, lanes), jnp.float32)
        for n in range(widths_ref.shape[0]):
            width = jnp.where(index == float(n), widths_ref[n], width)
        coef = -LOG2E / (2.0 * comps * width * width)
        total = jnp.zeros((8, lanes), jnp.float32)
        top = jnp.full((8, lanes), -BIG, jnp.float32)
        for n in range(len(keys)):
            inner = across(twice_ref[n], query)
            near = jnp.concatenate([near_ref[n]] * (lanes // 128), axis=1)
            wide = jnp.concatenate([wide_ref[n]] * (lanes // 128), axis=1)
            dist = jnp.maximum(inner + near + norm, 0.0)
            kernel = jnp.exp2(dist * coef)
            total = total + jnp.sum(kernel.reshape(share // 8, 8, lanes), axis=0)
            top = jnp.maximum(top, jnp.max((inner + wide).reshape(share // 8, 8, lanes), axis=0))
        out_ref[shard, 0:1, pl.ds(begin, lanes)] = jnp.sum(total, axis=0, keepdims=True)
        out_ref[shard, 1:2, pl.ds(begin, lanes)] = jnp.maximum(jnp.max(top, axis=0, keepdims=True) + norm, 0.0)

    for ref, flip in ((mine_ref, 0), (second_ref, 2), (beside_ref, 1), (across_ref, 3)):
        shard = jnp.bitwise_xor(where_ref[0], flip)
        for begin in range(0, share, lanes):
            step(ref, shard, begin)


def block_terms(where, fill, widths, mine, beside, own, far, other):
    share, comps = own.shape
    groups = len(mine) + len(beside)
    whole = pl.BlockSpec(memory_space=pltpu.VMEM)
    smem = pl.BlockSpec(memory_space=pltpu.SMEM)
    return pl.pallas_call(
        functools.partial(terms_kernel, share, comps),
        out_shape=jax.ShapeDtypeStruct((groups, 2, share), jnp.float32),
        in_specs=[smem] * 3 + [whole] * 7,
        out_specs=whole,
        scratch_shapes=[
            pltpu.VMEM((3, share, 128), jnp.float32),
            pltpu.VMEM((3, share, 128), jnp.float32),
            pltpu.VMEM((3, share, comps), jnp.bfloat16),
        ],
        compiler_params=pltpu.CompilerParams(vmem_limit_bytes=32 * 1024 * 1024),
    )(where, fill, widths, *mine, *beside, own, far, other)


def per_device(counts, loadings, kernel_widths, width_index, block_fill, plan):
    groups = lax.axis_size("gene")
    blocks = lax.axis_size("cell")
    rows = counts.shape[0]
    share = rows // groups
    gene_pos = lax.axis_index("gene")
    cell_pos = lax.axis_index("cell")
    comps = loadings.shape[1]
    far = blocks - 1
    first = gene_pos * share
    index = jnp.pad(width_index.reshape(-1, comps), ((0, EXTRA - share // comps), (0, 0)))

    def partial(shard):
        begin = jnp.bitwise_xor(gene_pos, shard) * share
        rows = lax.dynamic_slice_in_dim(counts, begin, share, 0)
        return jnp.dot(rows, loadings, preferred_element_type=jnp.float32)

    def narrow(x):
        return lax.reduce_precision(x, 8, 10).astype(jnp.float16)

    def widen(x):
        return x.astype(jnp.float32)

    near = swapped(narrow(partial(3)), "gene", 1)
    nearest = swapped(narrow(partial(1)), "gene", 1)
    theirs = narrow(partial(2) + widen(near))
    ours = partial(0) + widen(nearest)
    wide = swapped(theirs, "gene", 2)
    plan, ours = lax.optimization_barrier((plan, ours))
    other = jnp.where(plan[0] == far, plan[1], plan[0])
    where = jnp.stack([gene_pos, cell_pos, jnp.bitwise_xor(cell_pos, far), jnp.bitwise_xor(cell_pos, other)])
    forward = jnp.bitwise_and(other, 4) != 0
    path = jnp.where(forward, jnp.bitwise_xor(other, far), other)
    early = jnp.where(forward, 0, path % 4)
    late = jnp.where(forward, path % 4, 0)
    across_plane = path // 8
    wide, ours, forward, early, late, across_plane, where = lax.optimization_barrier((wide, ours, forward, early, late, across_plane, where))
    scores = (ours + widen(wide)).astype(jnp.bfloat16)
    mine = jnp.concatenate([scores, index.astype(jnp.bfloat16)])
    partner = swapped(scores, "cell", far)
    moved = chosen(scores, "cell", early, 1, 4)
    mine, moved = lax.optimization_barrier((mine, moved))
    across, second, beside = [swapped(mine, "gene", step) for step in (3, 2, 1)]
    mine = [mine, second]
    beside = [beside, across]
    moved = jnp.where(forward, partner, moved)
    moved = chosen(moved, "cell", late, 1, 4)
    moved = chosen(moved, "cell", across_plane, 8, blocks // 8)

    terms = block_terms(where, block_fill, kernel_widths, mine, beside, scores, partner, moved)
    both = lax.all_to_all(terms, "gene", 0, 0)
    total = jnp.sum(both[:, 0], axis=0)
    top = jnp.max(both[:, 1], axis=0)
    qlive = first + jnp.arange(share, dtype=jnp.int32) < block_fill[cell_pos]
    density = jnp.where(qlive, jnp.log(total), 0.0)
    spread = jnp.where(qlive, jnp.sqrt(top / comps), 0.0)
    return (density, spread)


def solution(mesh):
    placed = (P("cell", "gene"), P("gene", None), P(), P(("cell", "gene")), P(), P())
    return jax.shard_map(
        per_device,
        mesh=mesh,
        in_specs=placed,
        out_specs=(P(("cell", "gene")), P(("cell", "gene"))),
        check_vma=False,
    )
```

```python
import functools

import jax
import jax.numpy as jnp
from jax import lax
from jax.experimental import pallas as pl
from jax.experimental.pallas import tpu as pltpu
from jax.sharding import PartitionSpec as P

EXTRA = 16
BIG = 1e30
LOG2E = 1.4426950408889634


def swapped(value, axis, mask):
    pairs = [(source, source ^ mask) for source in range(lax.axis_size(axis))]
    return lax.ppermute(value, axis, pairs)


def chosen(value, axis, index, unit, count):
    moves = [lambda x: x]
    for step in range(1, count):
        moves.append(lambda x, mask=step * unit: swapped(x, axis, mask))
    return lax.switch(index, moves, value)


def squares(x):
    xf = x.astype(jnp.float32)
    square = xf * xf
    high = square.astype(jnp.bfloat16)
    low = (square - high.astype(jnp.float32)).astype(jnp.bfloat16)
    return high, low


def across(a, b):
    return lax.dot_general(a, b, (((1,), (1,)), ((), ())), preferred_element_type=jnp.float32)


def terms_kernel(share, comps, where_ref, fill_ref, widths_ref, mine_ref, second_ref, beside_ref, across_ref, own_ref, far_ref, other_ref, out_ref, near_ref, wide_ref, twice_ref):
    first = where_ref[0] * share
    keys = (own_ref, far_ref, other_ref)
    ones = jnp.ones((128, comps), jnp.bfloat16)
    slot = first + lax.broadcasted_iota(jnp.int32, (share, 128), 0)
    for n, key_ref in enumerate(keys):
        block = key_ref[...]
        high, low = squares(block)
        norm = across(high, ones) + across(low, ones)
        live = slot < fill_ref[where_ref[1 + n]]
        near_ref[n] = jnp.where(live, norm, BIG)
        wide_ref[n] = jnp.where(live, norm, -BIG)
        twice_ref[n] = block * jnp.bfloat16(-2)

    lanes = 256
    def step(query_ref, shard, begin):
        query = query_ref[pl.ds(begin, lanes), :]
        high, low = squares(query)
        few = jnp.ones((8, comps), jnp.bfloat16)
        norm = (across(few, high) + across(few, low))[:1]
        index = query_ref[share:, :].astype(jnp.float32)
        index = jnp.concatenate([index[row : row + 1] for row in range(begin // comps, (begin + lanes) // comps)], axis=1)
        width = jnp.zeros((1, lanes), jnp.float32)
        for n in range(widths_ref.shape[0]):
            width = jnp.where(index == float(n), widths_ref[n], width)
        coef = -LOG2E / (2.0 * comps * width * width)
        total = jnp.zeros((8, lanes), jnp.float32)
        top = jnp.full((8, lanes), -BIG, jnp.float32)
        for n in range(len(keys)):
            inner = across(twice_ref[n], query)
            near = jnp.concatenate([near_ref[n]] * (lanes // 128), axis=1)
            wide = jnp.concatenate([wide_ref[n]] * (lanes // 128), axis=1)
            dist = jnp.maximum(inner + near + norm, 0.0)
            kernel = jnp.exp2(dist * coef)
            total = total + jnp.sum(kernel.reshape(share // 8, 8, lanes), axis=0)
            top = jnp.maximum(top, jnp.max((inner + wide).reshape(share // 8, 8, lanes), axis=0))
        out_ref[shard, 0:1, pl.ds(begin, lanes)] = jnp.sum(total, axis=0, keepdims=True)
        out_ref[shard, 1:2, pl.ds(begin, lanes)] = jnp.maximum(jnp.max(top, axis=0, keepdims=True) + norm, 0.0)

    for ref, flip in ((mine_ref, 0), (second_ref, 2), (beside_ref, 1), (across_ref, 3)):
        shard = jnp.bitwise_xor(where_ref[0], flip)
        for begin in range(0, share, lanes):
            step(ref, shard, begin)


def block_terms(where, fill, widths, mine, beside, own, far, other):
    share, comps = own.shape
    groups = len(mine) + len(beside)
    whole = pl.BlockSpec(memory_space=pltpu.VMEM)
    smem = pl.BlockSpec(memory_space=pltpu.SMEM)
    return pl.pallas_call(
        functools.partial(terms_kernel, share, comps),
        out_shape=jax.ShapeDtypeStruct((groups, 2, share), jnp.float32),
        in_specs=[smem] * 3 + [whole] * 7,
        out_specs=whole,
        scratch_shapes=[
            pltpu.VMEM((3, share, 128), jnp.float32),
            pltpu.VMEM((3, share, 128), jnp.float32),
            pltpu.VMEM((3, share, comps), jnp.bfloat16),
        ],
        compiler_params=pltpu.CompilerParams(vmem_limit_bytes=32 * 1024 * 1024),
    )(where, fill, widths, *mine, *beside, own, far, other)


def per_device(counts, loadings, kernel_widths, width_index, block_fill, plan):
    groups = lax.axis_size("gene")
    blocks = lax.axis_size("cell")
    rows = counts.shape[0]
    share = rows // groups
    gene_pos = lax.axis_index("gene")
    cell_pos = lax.axis_index("cell")
    comps = loadings.shape[1]
    far = blocks - 1
    first = gene_pos * share
    index = jnp.pad(width_index.reshape(-1, comps), ((0, EXTRA - share // comps), (0, 0)))

    def partial(shard):
        begin = jnp.bitwise_xor(gene_pos, shard) * share
        rows = lax.dynamic_slice_in_dim(counts, begin, share, 0)
        return jnp.dot(rows, loadings, preferred_element_type=jnp.float32)

    def narrow(x):
        return lax.reduce_precision(x, 8, 10).astype(jnp.float16)

    def widen(x):
        return x.astype(jnp.float32)

    near = swapped(narrow(partial(3)), "gene", 1)
    nearest = swapped(narrow(partial(1)), "gene", 1)
    near, held = lax.optimization_barrier((near, partial(2)))
    theirs = narrow(held + widen(near))
    ours = partial(0) + widen(nearest)
    wide = swapped(theirs, "gene", 2)
    plan, ours = lax.optimization_barrier((plan, ours))
    other = jnp.where(plan[0] == far, plan[1], plan[0])
    where = jnp.stack([gene_pos, cell_pos, jnp.bitwise_xor(cell_pos, far), jnp.bitwise_xor(cell_pos, other)])
    forward = jnp.bitwise_and(other, 4) != 0
    path = jnp.where(forward, jnp.bitwise_xor(other, far), other)
    early = jnp.where(forward, 0, path % 4)
    late = jnp.where(forward, path % 4, 0)
    across_plane = path // 8
    wide, ours, forward, early, late, across_plane, where = lax.optimization_barrier((wide, ours, forward, early, late, across_plane, where))
    scores = (ours + widen(wide)).astype(jnp.bfloat16)
    mine = jnp.concatenate([scores, index.astype(jnp.bfloat16)])
    partner = swapped(scores, "cell", far)
    moved = chosen(scores, "cell", early, 1, 4)
    beside = swapped(mine, "gene", 1)
    again, moved = lax.optimization_barrier((mine, moved))
    across, second = [swapped(again, "gene", step) for step in (3, 2)]
    mine = [mine, second]
    beside = [beside, across]
    moved = jnp.where(forward, partner, moved)
    moved = chosen(moved, "cell", late, 1, 4)
    moved = chosen(moved, "cell", across_plane, 8, blocks // 8)

    terms = block_terms(where, block_fill, kernel_widths, mine, beside, scores, partner, moved)
    both = lax.all_to_all(terms, "gene", 0, 0)
    total = jnp.sum(both[:, 0], axis=0)
    top = jnp.max(both[:, 1], axis=0)
    qlive = first + jnp.arange(share, dtype=jnp.int32) < block_fill[cell_pos]
    density = jnp.where(qlive, jnp.log(total), 0.0)
    spread = jnp.where(qlive, jnp.sqrt(top / comps), 0.0)
    return (density, spread)


def solution(mesh):
    placed = (P("cell", "gene"), P("gene", None), P(), P(("cell", "gene")), P(), P())
    return jax.shard_map(
        per_device,
        mesh=mesh,
        in_specs=placed,
        out_specs=(P(("cell", "gene")), P(("cell", "gene"))),
        check_vma=False,
    )
```
